32 devices in a mesh: groups: 2 (over y), outer: 2 (over core), inner: 8 (over z, x).
Axes of the slice: x: 2, y: 2, z: 4, core: 2. Of those that a mesh axis runs over, the one named last changes fastest.
Arguments:
- readings: float32 [2048, 16384], P(('groups', 'outer'), 'inner'), parts along dimension 0, may hold values from -6 to 6
- obs_rows: float32 [16384, 16], replicated, may hold values from -0.1875 to 0.1875
- obs_block: int32 [16384], replicated, may hold values from 0 to 15
- sensor_prec: float32 [16384], replicated, may hold values from 0.2 to 5
- prior_mean: float32 [512], P('groups'), parts along dimension 0, may hold values from -5 to 5
- filt_trans: float32 [256, 256], replicated, may hold values from -1 to 1
- model_trans: float32 [256, 256], replicated, may hold values from -1 to 1
- info_gain: float32 [256, 256], replicated, may hold values from -0.01171875 to 0.01171875
- smooth_gain: float32 [256, 256], replicated, may hold values from -1 to 1
Outputs:
- filtered: float32 [2048, 256], P(('groups', 'outer', 'inner')), parts along dimension 0
- smoothed: float32 [2048, 256], P(('groups', 'outer', 'inner')), parts along dimension 0
The draws below stay inside these ranges and needn't reach their ends.
There are 2 independent parts, one for each index of `groups`. The reference program is written for one: setup_inputs(seed, part) draws one part's arguments, and reference() takes and returns one part's arrays. A program takes and returns all parts, laid end to end along the dimension named above; an argument that names none is the same for every part. Nothing has to cross between parts.
All inputs are finite; a program needn't handle non-finite values.
Results may differ from the reference program's by a relative error of at most 0.0003.
Values sent between devices are 32-bit elements; how exact they have to be, the bound alone decides.
A program may use at most 256 MiB of HBM per device.

```python
import math
import jax
import jax.numpy as jnp
from jax import lax

NS = 256
BLK = 16
SENSORS = 16384
STEPS = 1024


def spectral_matrix(key, slow_low, slow_high):
    sign_key, rate_key, angle_key, scale_key = jax.random.split(key, 4)
    row_index = jnp.arange(NS, dtype=jnp.float32)[:, None]
    col_index = jnp.arange(NS, dtype=jnp.float32)[None, :]
    cos_basis = jnp.cos(jnp.pi * (row_index + 0.5) * col_index / NS) * jnp.sqrt(2.0 / NS)
    cos_basis = jnp.where(col_index == 0, jnp.sqrt(1.0 / NS), cos_basis)
    sign_flip = jnp.where(jax.random.bernoulli(sign_key, 0.5, (NS, 1)), 1.0, -1.0)
    rotated = sign_flip * cos_basis
    pair_count = NS // 2
    pair_rates = jax.random.uniform(rate_key, (pair_count,), jnp.float32, jnp.log(slow_low), jnp.log(slow_high))
    radius = 1.0 - jnp.exp(pair_rates)
    angles = jax.random.uniform(angle_key, (pair_count,), jnp.float32, 0.003, 0.03)
    cos_part = (radius * jnp.cos(angles))[None, :]
    sin_part = (radius * jnp.sin(angles))[None, :]
    paired = rotated.reshape(NS, pair_count, 2)
    even_cols = paired[:, :, 0]
    odd_cols = paired[:, :, 1]
    new_even = even_cols * cos_part + odd_cols * sin_part
    new_odd = odd_cols * cos_part - even_cols * sin_part
    turned = jnp.stack([new_even, new_odd], axis=2).reshape(NS, NS)
    core = jnp.dot(turned, rotated.T, precision=lax.Precision.HIGHEST)
    diag_scale = jnp.exp(jax.random.uniform(scale_key, (NS,), jnp.float32, -0.35, 0.35))
    return core * diag_scale[:, None] / diag_scale[None, :]


def draw_filt_trans(key, part):
    key = jax.random.fold_in(key, 11)
    return spectral_matrix(key, 0.0001, 0.05)


def draw_model_trans(key, part):
    key = jax.random.fold_in(key, 37)
    return spectral_matrix(key, 0.0001, 0.05)


def draw_smooth_gain(key, part):
    key = jax.random.fold_in(key, 23)
    return spectral_matrix(key, 0.0001, 0.05)


def with_ends(entries, key, smallest, top_value):
    longest = entries.shape.index(max(entries.shape))
    spots = []
    for shift in (0, 1):
        where = [jax.random.randint(jax.random.fold_in(key, axis), (), 0, length) for axis, length in enumerate(entries.shape)]
        where[longest] = (where[longest] + shift) % entries.shape[longest]
        spots.append(tuple(where))
    return entries.at[spots[0]].set(smallest).at[spots[1]].set(top_value)


def block_levels(key, shape, cuts, least, largest):
    gain, own = 1.0, jax.random.fold_in(key, 6)
    for dim, parts in cuts:
        draws = jnp.exp(jax.random.uniform(jax.random.fold_in(own, dim), (parts,), jnp.float32, least / len(cuts), largest / len(cuts)))
        gain = gain * jnp.repeat(draws, shape[dim] // parts).reshape([-1 if axis == dim else 1 for axis in range(len(shape))])
    return gain


def centred(rng, shape, spread, most, cuts=(), held_as=jnp.bfloat16):
    drawn = spread * jax.random.normal(rng, shape, jnp.float32)
    if cuts:
        drawn = drawn * block_levels(rng, shape, cuts, -0.22, 0.18)
    return jnp.clip(drawn, -most, most).astype(held_as)


def setup_inputs(seed: int = 0, part: int = 0) -> dict:
    key_of = jax.random.split(jax.random.key(seed), 10)
    own_keys = jax.random.split(jax.random.fold_in(key_of[9], part), 10)
    return {
        "readings": centred(own_keys[0], (STEPS, SENSORS), 1.0, 6.0, ((0, 2), (1, 8)), jnp.float32),
        "obs_rows": centred(key_of[1], (SENSORS, BLK), (SENSORS * BLK // NS) ** -0.5, 0.1875, (), jnp.float32),
        "obs_block": with_ends(jax.random.randint(key_of[2], (SENSORS,), 0, NS // BLK), jax.random.fold_in(key_of[2], 1), 0, (NS // BLK) - 1).astype(jnp.int32),
        "sensor_prec": jnp.clip(jnp.exp(jax.random.uniform(key_of[3], (SENSORS,), jnp.float32, math.log(0.2), math.log(5.0))), 0.2, 5.0),
        "prior_mean": centred(own_keys[4], (NS,), 1.0, 5.0, (), jnp.float32),
        "filt_trans": draw_filt_trans(jax.random.fold_in(key_of[9], 71), part),
        "model_trans": draw_model_trans(jax.random.fold_in(key_of[9], 71), part),
        "info_gain": centred(key_of[7], (NS, NS), (NS * 1000) ** -0.5, 0.01171875, (), jnp.float32),
        "smooth_gain": draw_smooth_gain(jax.random.fold_in(key_of[9], 71), part),
    }


highest = lax.Precision.HIGHEST


def reference(readings, obs_rows, obs_block, sensor_prec, prior_mean, filt_trans, model_trans, info_gain, smooth_gain):
    blocks = NS // BLK
    one_hot = (obs_block[:, None] == jnp.arange(blocks, dtype=jnp.int32)[None, :]).astype(jnp.float32)
    obs_full = (one_hot[:, :, None] * obs_rows[:, None, :]).reshape(SENSORS, NS)
    weighted = readings * sensor_prec[None, :]
    information = jnp.dot(weighted, obs_full, precision=highest)
    drives = jnp.dot(information, info_gain.T, precision=highest)

    def advance(carried, drive_row):
        updated = jnp.dot(filt_trans, carried, precision=highest) + drive_row
        return updated, updated

    final_state, filtered = lax.scan(advance, prior_mean, drives)
    predicted = jnp.dot(jnp.dot(filtered, model_trans.T, precision=highest), smooth_gain.T, precision=highest)
    last_row = (jnp.arange(STEPS, dtype=jnp.int32) == STEPS - 1)[:, None]
    corrections = jnp.where(last_row, filtered, filtered - predicted)

    def retreat(carried, correction_row):
        updated = jnp.dot(smooth_gain, carried, precision=highest) + correction_row
        return updated, updated

    first_state, smoothed = lax.scan(retreat, jnp.zeros((NS,), jnp.float32), corrections, reverse=True)
    return filtered, smoothed
```

```python
import functools

import jax
import jax.numpy as jnp
from jax import lax
from jax.experimental import pallas as pl
from jax.experimental.pallas import tpu as pltpu
from jax.sharding import PartitionSpec as P

MESH = pl.DeviceIdType.MESH
F32 = jnp.float32
BF16 = jnp.bfloat16
KU, KQ, KD, KP, KW = range(5)
MGAIN, MCORR, MEXIT, MMODEL, MWIN = range(5)


def split(x):
    high = x.astype(BF16)
    low = (x - high.astype(F32)).astype(BF16)
    return high, low


def dot(a, b):
    return jnp.dot(a, b, preferred_element_type=F32)


def dot3(a, b):
    return dot(a[0], b[0]) + (dot(a[1], b[0]) + dot(a[0], b[1]))


def exact(a, b):
    return jnp.dot(a, b, precision=lax.Precision.HIGHEST, preferred_element_type=F32)


def first_rows(x, m):
    return jnp.where(lax.broadcasted_iota(jnp.int32, x.shape, 0) < m, x, 0.0)


def halves(x, m):
    if m >= 16:
        return x[:m], x[m:]
    return first_rows(x, m), first_rows(pltpu.roll(x, 16 - m, 0), m)


def stack(top, below, m):
    if m >= 16:
        return jnp.concatenate([top, below], axis=0)
    return top + pltpu.roll(below, m, 0)


def shift_down(x, k):
    return jnp.concatenate([jnp.zeros((k, x.shape[1]), F32), x[:-k]], axis=0)


def shift_up(x, k):
    return jnp.concatenate([x[k:], jnp.zeros((k, x.shape[1]), F32)], axis=0)


def bit_reversed(t, bits):
    return int(format(t, "0%db" % bits)[::-1], 2) if bits else 0


def kernel(
    n_out, n_in, readings, obs_t, block, prec, prior, filt, model, gain, smooth,
    filtered, smoothed,
    chunk, obs_v, obs_w, part, landed, info, lev, dev, misc, pf, qf, wf, mine, ends, pick, kept, leaf,
    in_sem, obs_sem, send_sem, recv_sem, esend_sem, erecv_sem,
):
    n = n_out * n_in
    steps, ns = filtered.shape
    sensors = obs_v.shape[1]
    blk = obs_v.shape[0]
    levels = steps.bit_length() - 1
    dev_levels = n.bit_length() - 1
    inner = lax.axis_index("inner")
    place = lax.axis_index("outer") * n_in + inner

    def target(k):
        q = lax.rem(place + k, n)
        return {"outer": q // n_in, "inner": lax.rem(q, n_in)}

    barrier = pltpu.get_barrier_semaphore()

    def greet(k, c):
        pl.semaphore_signal(barrier, inc=1, device_id=target(k), device_id_type=MESH)
        return c

    lax.fori_loop(1, n, greet, 0)

    obs_copy = pltpu.make_async_copy(
        obs_t.at[:, pl.ds(pl.multiple_of(inner * sensors, sensors), sensors)], obs_v, obs_sem
    )
    obs_copy.start()

    def in_copy(k):
        dest = lax.rem(inner + k + 1, n_in)
        return pltpu.make_async_copy(
            readings.at[pl.ds(pl.multiple_of(dest * steps, steps), steps), :],
            chunk.at[k],
            in_sem.at[k],
        )

    def start_in(k, c):
        in_copy(k).start()
        return c

    lax.fori_loop(0, n_in, start_in, 0)
    obs_copy.wait()

    per_row = sensors // 128

    def lane_row(ref):
        return jnp.concatenate(
            [ref[pl.ds(inner * per_row + r, 1), :] for r in range(per_row)], axis=1
        )

    scaled = obs_v[...] * lane_row(prec)
    which = lane_row(block)
    for b in range(ns // blk):
        high, low = split(jnp.where(which == b, scaled, 0.0))
        obs_w[0, b * blk : (b + 1) * blk, :] = high
        obs_w[1, b * blk : (b + 1) * blk, :] = low

    def nt(a, b):
        return lax.dot_general(a, b, (((1,), (1,)), ((), ())), preferred_element_type=F32)

    def rs_copy(k):
        return pltpu.make_async_remote_copy(
            src_ref=part.at[k],
            dst_ref=landed.at[k],
            send_sem=send_sem.at[k],
            recv_sem=recv_sem.at[k],
            device_id={"inner": lax.rem(inner + k + 1, n_in)},
            device_id_type=MESH,
        )

    def partial_sum(k):
        in_copy(k).wait()
        high, low = split(chunk[k])
        part[k] = nt(high, obs_w[0]) + (nt(low, obs_w[0]) + nt(high, obs_w[1]))

    pl.semaphore_wait(barrier, n - 1)

    def reduce_step(k, c):
        partial_sum(k)
        rs_copy(k).start()
        return c

    lax.fori_loop(0, n_in - 1, reduce_step, 0)
    partial_sum(n_in - 1)

    def put(ref, where, value):
        high, low = split(value)
        ref[where + (0,)] = high
        ref[where + (1,)] = low

    trans = filt[...].T
    back = smooth[...].T
    model_t = model[...].T
    put(misc, (MGAIN,), gain[...].T)
    put(misc, (MMODEL,), model_t)
    corr = -exact(model_t, back)
    eye = (
        lax.broadcasted_iota(jnp.int32, (ns, ns), 0) == lax.broadcasted_iota(jnp.int32, (ns, ns), 1)
    )
    corr = jnp.where(eye, corr + 1.0, corr)
    put(misc, (MCORR,), corr)
    pf[...] = trans
    qf[...] = back
    wf[...] = exact(trans, corr)
    start = exact(jnp.broadcast_to(prior[...], (16, ns)), trans)[0:1]

    def grow(k, c):
        p, q, w = pf[...], qf[...], wf[...]
        p2, q2, w2 = split(p), split(q), split(w)
        d2 = split(dot3(p2, w2))
        for kind, pair in ((KU, split(dot3(w2, q2))), (KQ, q2), (KD, d2), (KP, p2), (KW, w2)):
            lev[k, 0, kind * ns : (kind + 1) * ns, :] = pair[0]
            lev[k, 1, kind * ns : (kind + 1) * ns, :] = pair[1]
        wf[...] = w + dot3(d2, q2)
        pf[...] = exact(p, p)
        qf[...] = exact(q, q)
        return c

    lax.fori_loop(0, levels, grow, 0)
    put(misc, (MWIN,), wf[...])
    put(misc, (MEXIT,), exact(model_t, qf[...]))

    def grow_dev(k, c):
        p, q = pf[...], qf[...]
        put(dev, (k, 0), p)
        put(dev, (k, 1), q)
        pf[...] = exact(p, p)
        qf[...] = exact(q, q)
        return c

    lax.fori_loop(0, dev_levels, grow_dev, 0)

    def mul(x2, ref, *where):
        return dot3(x2, (ref[where + (0,)], ref[where + (1,)]))

    def step(x2, k, kind):
        here = slice(kind * ns, kind * ns + x2[0].shape[1])
        return dot3(x2, (lev[k, 0, here, :], lev[k, 1, here, :]))

    def beside(a, b):
        return tuple(jnp.concatenate([u, v], axis=1) for u, v in zip(a, b))

    info[...] = part[n_in - 1]

    def take(k, c):
        rs_copy(k).wait_recv()
        info[...] += landed[k]
        return c

    lax.fori_loop(0, n_in - 1, take, 0)
    drive = mul(split(info[...]), misc, MGAIN)
    first = jnp.where(place == 0, 1.0, 0.0)
    top = lax.broadcasted_iota(jnp.int32, (steps, 1), 0) == 0
    drive = drive + jnp.where(jnp.logical_and(top, first > 0.5), start, 0.0)
    info[...] = drive
    for t in range(steps):
        r = bit_reversed(t, levels)
        leaf[0, r : r + 1, :] = info[t : t + 1, :]
    leaf[1] = mul(split(leaf[0]), misc, MCORR)
    drive, head = leaf[0], leaf[1]

    e, h = drive, head
    spot = [0]
    for k in range(levels):
        m = steps >> (k + 1)
        (el, er), (hl, hr) = halves(e, m), halves(h, m)
        el2, hr2 = split(el), split(hr)
        e = er + step(el2, k, KP)
        h = hl + step(beside(el2, hr2), k, KU)
        here = pl.ds(spot[-1], el.shape[0])
        kept[0, here, :] = el
        kept[1, here, :] = hr + step(el2, k, KW)
        spot.append(spot[-1] + el.shape[0])

    half = ns // 2
    for ref in (mine, ends.at[place]):
        ref[0:1, :] = e[0:1, :half]
        ref[1:2, :] = e[0:1, half:]
        ref[2:3, :] = h[0:1, :half]
        ref[3:4, :] = h[0:1, half:]

    def end_copy(k):
        return pltpu.make_async_remote_copy(
            src_ref=mine,
            dst_ref=ends.at[place],
            send_sem=esend_sem.at[k],
            recv_sem=erecv_sem.at[k],
            device_id=target(k),
            device_id_type=MESH,
        )

    def end_arrival(k):
        q = lax.rem(place - k + n, n)
        return pltpu.make_async_remote_copy(
            src_ref=mine,
            dst_ref=ends.at[q],
            send_sem=esend_sem.at[k],
            recv_sem=erecv_sem.at[k],
            device_id=target(k),
            device_id_type=MESH,
        )

    def send_end(k, c):
        end_copy(k).start()
        return c

    lax.fori_loop(1, n, send_end, 0)

    def take_end(k, c):
        end_arrival(k).wait_recv()
        return c

    lax.fori_loop(1, n, take_end, 0)

    x = jnp.concatenate([ends[:, 0, :], ends[:, 1, :]], axis=1)
    s = jnp.concatenate([ends[:, 2, :], ends[:, 3, :]], axis=1)
    for k in range(dev_levels):
        x = x + shift_down(mul(split(x), dev, k, 0), 1 << k)
    x2 = split(x)
    last = lax.broadcasted_iota(jnp.int32, (n, 1), 0) == n - 1
    s = s + shift_down(mul(x2, misc, MWIN), 1) + jnp.where(last, mul(x2, misc, MEXIT), 0.0)
    for k in range(dev_levels):
        s = s + shift_up(mul(split(s), dev, k, 1), 1 << k)
    pick[0] = shift_down(x, 1)
    pick[1] = jnp.where(last, mul(x2, misc, MMODEL), shift_up(s, 1))
    x = first_rows(jnp.broadcast_to(pick[0, pl.ds(place, 1), :], (16, ns)), 1)
    s = first_rows(jnp.broadcast_to(pick[1, pl.ds(place, 1), :], (16, ns)), 1)

    for k in range(levels - 1, -1, -1):
        m = steps >> (k + 1)
        here = pl.ds(spot[k], spot[k + 1] - spot[k])
        el, g = kept[0, here, :], kept[1, here, :]
        x2, s2 = split(x), split(s)
        xr = el + step(x2, k, KP)
        sl = g + step(beside(s2, x2), k, KQ)
        x = stack(x, xr, m)
        s = stack(sl, s, m)
    x2 = split(x)
    f_rows = leaf[0] + step(x2, 0, KP)
    s_rows = leaf[1] + (step(x2, 0, KW) + step(split(s), 0, KQ))
    for t in range(steps):
        r = bit_reversed(t, levels)
        filtered[t : t + 1, :] = f_rows[r : r + 1, :]
        smoothed[t : t + 1, :] = s_rows[r : r + 1, :]

    def drain(k, c):
        rs_copy(k).wait_send()
        return c

    lax.fori_loop(0, n_in - 1, drain, 0)

    def drain_end(k, c):
        end_copy(k).wait_send()
        return c

    lax.fori_loop(1, n, drain_end, 0)


def on_device(
    readings, obs_rows, obs_block, sensor_prec, prior_mean, filt_trans, model_trans, info_gain, smooth_gain
):
    n_out, n_in = lax.axis_size("outer"), lax.axis_size("inner")
    n = n_out * n_in
    rows, sensors = readings.shape
    steps = rows // n_in
    ns = filt_trans.shape[0]
    blk = obs_rows.shape[1]
    total = obs_rows.shape[0]
    levels = steps.bit_length() - 1
    dev_levels = n.bit_length() - 1
    vmem = pl.BlockSpec(memory_space=pltpu.VMEM)
    hbm = pl.BlockSpec(memory_space=pl.ANY)
    dma = pltpu.SemaphoreType.DMA
    return pl.pallas_call(
        functools.partial(kernel, n_out, n_in),
        out_shape=[jax.ShapeDtypeStruct((steps, ns), F32)] * 2,
        in_specs=[hbm, hbm] + [vmem] * 7,
        out_specs=[vmem, vmem],
        scratch_shapes=[
            pltpu.VMEM((n_in, steps, sensors), F32),
            pltpu.VMEM((blk, sensors), F32),
            pltpu.VMEM((2, ns, sensors), BF16),
            pltpu.VMEM((n_in, steps, ns), F32),
            pltpu.VMEM((n_in - 1, steps, ns), F32),
            pltpu.VMEM((steps, ns), F32),
            pltpu.VMEM((levels, 2, 5 * ns, ns), BF16),
            pltpu.VMEM((dev_levels, 2, 2, ns, ns), BF16),
            pltpu.VMEM((5, 2, ns, ns), BF16),
            pltpu.VMEM((ns, ns), F32),
            pltpu.VMEM((ns, ns), F32),
            pltpu.VMEM((ns, ns), F32),
            pltpu.VMEM((8, ns // 2), F32),
            pltpu.VMEM((n, 8, ns // 2), F32),
            pltpu.VMEM((2, n, ns), F32),
            pltpu.VMEM((2, steps + 16 * levels, ns), F32),
            pltpu.VMEM((2, steps, ns), F32),
            dma((n_in,)),
            dma(()),
            dma((n_in - 1,)),
            dma((n_in - 1,)),
            dma((n,)),
            dma((n,)),
        ],
        compiler_params=pltpu.CompilerParams(
            collective_id=0, has_side_effects=True, vmem_limit_bytes=56 * 1024 * 1024
        ),
        name="smoother",
    )(
        readings,
        obs_rows.T,
        obs_block.reshape(total // 128, 128),
        sensor_prec.reshape(total // 128, 128),
        prior_mean.reshape(1, ns),
        filt_trans,
        model_trans,
        info_gain,
        smooth_gain,
    )


def solution(mesh):
    placed = (P(("groups", "outer"), "inner"), P(), P(), P(), P("groups"), P(), P(), P(), P())
    return jax.shard_map(
        on_device,
        mesh=mesh,
        in_specs=placed,
        out_specs=(P(("groups", "outer", "inner"), None), P(("groups", "outer", "inner"), None)),
        check_vma=False,
    )
```

```python
import functools

import jax
import jax.numpy as jnp
from jax import lax
from jax.experimental import pallas as pl
from jax.experimental.pallas import tpu as pltpu
from jax.sharding import PartitionSpec as P

MESH = pl.DeviceIdType.MESH
F32 = jnp.float32
BF16 = jnp.bfloat16
KU, KQ, KD, KP, KW = range(5)
MGAIN, MCORR, MEXIT, MMODEL, MWIN = range(5)


def split(x):
    high = x.astype(BF16)
    low = (x - high.astype(F32)).astype(BF16)
    return high, low


def dot(a, b):
    return jnp.dot(a, b, preferred_element_type=F32)


def dot3(a, b):
    return dot(a[0], b[0]) + (dot(a[1], b[0]) + dot(a[0], b[1]))


def exact(a, b):
    return jnp.dot(a, b, precision=lax.Precision.HIGHEST, preferred_element_type=F32)


def first_rows(x, m):
    return jnp.where(lax.broadcasted_iota(jnp.int32, x.shape, 0) < m, x, 0.0)


def halves(x, m):
    if m >= 16:
        return x[:m], x[m:]
    return first_rows(x, m), first_rows(pltpu.roll(x, 16 - m, 0), m)


def stack(top, below, m):
    if m >= 16:
        return jnp.concatenate([top, below], axis=0)
    return top + pltpu.roll(below, m, 0)


def shift_down(x, k):
    return jnp.concatenate([jnp.zeros((k, x.shape[1]), F32), x[:-k]], axis=0)


def shift_up(x, k):
    return jnp.concatenate([x[k:], jnp.zeros((k, x.shape[1]), F32)], axis=0)


def bit_reversed(t, bits):
    return int(format(t, "0%db" % bits)[::-1], 2) if bits else 0


def kernel(
    n_out, n_in, readings, obs_t, block, prec, prior, filt, model, gain, smooth,
    filtered, smoothed,
    chunk, obs_v, obs_w, part, landed, info, lev, dev, misc, pf, qf, wf, mine, ends, pick, kept, leaf,
    in_sem, obs_sem, send_sem, recv_sem, esend_sem, erecv_sem,
):
    n = n_out * n_in
    steps, ns = filtered.shape
    sensors = obs_v.shape[1]
    blk = obs_v.shape[0]
    levels = steps.bit_length() - 1
    dev_levels = n.bit_length() - 1
    inner = lax.axis_index("inner")
    place = lax.axis_index("outer") * n_in + inner

    def target(k):
        q = lax.rem(place + k, n)
        return {"outer": q // n_in, "inner": lax.rem(q, n_in)}

    barrier = pltpu.get_barrier_semaphore()

    def greet(k, c):
        pl.semaphore_signal(barrier, inc=1, device_id=target(k), device_id_type=MESH)
        return c

    lax.fori_loop(1, n, greet, 0)

    obs_copy = pltpu.make_async_copy(
        obs_t.at[:, pl.ds(pl.multiple_of(inner * sensors, sensors), sensors)], obs_v, obs_sem
    )
    obs_copy.start()

    def in_copy(k):
        dest = lax.rem(inner + k + 1, n_in)
        return pltpu.make_async_copy(
            readings.at[pl.ds(pl.multiple_of(dest * steps, steps), steps), :],
            chunk.at[k],
            in_sem.at[k],
        )

    def start_in(k, c):
        in_copy(k).start()
        return c

    lax.fori_loop(0, n_in, start_in, 0)
    obs_copy.wait()

    per_row = sensors // 128

    def lane_row(ref):
        return jnp.concatenate(
            [ref[pl.ds(inner * per_row + r, 1), :] for r in range(per_row)], axis=1
        )

    scaled = obs_v[...] * lane_row(prec)
    which = lane_row(block)
    for col in range(0, sensors, 256):
        here = slice(col, col + 256)
        wide = jnp.concatenate(
            [jnp.where(which[:, here] == b, scaled[:, here], 0.0) for b in range(ns // blk)], axis=0
        )
        high, low = split(wide.T)
        obs_w[0, here, :] = high
        obs_w[1, here, :] = low

    def nt(a, b):
        return dot(a, b)

    def rs_copy(k):
        return pltpu.make_async_remote_copy(
            src_ref=part.at[k],
            dst_ref=landed.at[k],
            send_sem=send_sem.at[k],
            recv_sem=recv_sem.at[k],
            device_id={"inner": lax.rem(inner + k + 1, n_in)},
            device_id_type=MESH,
        )

    def partial_sum(k):
        in_copy(k).wait()
        in_copy(k + 1).wait()
        high, low = split(chunk[pl.ds(k, 2)].reshape(2 * steps, sensors))
        both = nt(high, obs_w[0]) + (nt(low, obs_w[0]) + nt(high, obs_w[1]))
        part[k] = both[:steps]
        part[k + 1] = both[steps:]

    pl.semaphore_wait(barrier, n - 1)

    def reduce_step(j, c):
        partial_sum(2 * j)
        rs_copy(2 * j).start()
        rs_copy(2 * j + 1).start()
        return c

    lax.fori_loop(0, n_in // 2 - 1, reduce_step, 0)
    partial_sum(n_in - 2)
    rs_copy(n_in - 2).start()

    def put(ref, where, value):
        high, low = split(value)
        ref[where + (0,)] = high
        ref[where + (1,)] = low

    trans = filt[...].T
    back = smooth[...].T
    model_t = model[...].T
    put(misc, (MGAIN,), gain[...].T)
    put(misc, (MMODEL,), model_t)
    corr = -exact(model_t, back)
    eye = (
        lax.broadcasted_iota(jnp.int32, (ns, ns), 0) == lax.broadcasted_iota(jnp.int32, (ns, ns), 1)
    )
    corr = jnp.where(eye, corr + 1.0, corr)
    put(misc, (MCORR,), corr)
    pf[...] = trans
    qf[...] = back
    wf[...] = exact(trans, corr)
    start = exact(jnp.broadcast_to(prior[...], (16, ns)), trans)[0:1]

    def grow(k, c):
        p, q, w = pf[...], qf[...], wf[...]
        p2, q2, w2 = split(p), split(q), split(w)
        d2 = split(dot3(p2, w2))
        for kind, pair in ((KU, split(dot3(w2, q2))), (KQ, q2), (KD, d2), (KP, p2), (KW, w2)):
            lev[k, 0, kind * ns : (kind + 1) * ns, :] = pair[0]
            lev[k, 1, kind * ns : (kind + 1) * ns, :] = pair[1]
        wf[...] = w + dot3(d2, q2)
        pf[...] = exact(p, p)
        qf[...] = exact(q, q)
        return c

    lax.fori_loop(0, levels, grow, 0)
    put(misc, (MWIN,), wf[...])
    put(misc, (MEXIT,), exact(model_t, qf[...]))

    def grow_dev(k, c):
        p, q = pf[...], qf[...]
        put(dev, (k, 0), p)
        put(dev, (k, 1), q)
        pf[...] = exact(p, p)
        qf[...] = exact(q, q)
        return c

    lax.fori_loop(0, dev_levels, grow_dev, 0)

    def mul(x2, ref, *where):
        return dot3(x2, (ref[where + (0,)], ref[where + (1,)]))

    def step(x2, k, kind):
        here = slice(kind * ns, kind * ns + x2[0].shape[1])
        return dot3(x2, (lev[k, 0, here, :], lev[k, 1, here, :]))

    def beside(a, b):
        return tuple(jnp.concatenate([u, v], axis=1) for u, v in zip(a, b))

    info[...] = part[n_in - 1]

    def take(k, c):
        rs_copy(k).wait_recv()
        info[...] += landed[k]
        return c

    lax.fori_loop(0, n_in - 1, take, 0)
    drive = mul(split(info[...]), misc, MGAIN)
    first = jnp.where(place == 0, 1.0, 0.0)
    top = lax.broadcasted_iota(jnp.int32, (steps, 1), 0) == 0
    drive = drive + jnp.where(jnp.logical_and(top, first > 0.5), start, 0.0)
    info[...] = drive
    for t in range(steps):
        r = bit_reversed(t, levels)
        leaf[0, r : r + 1, :] = info[t : t + 1, :]
    leaf[1] = mul(split(leaf[0]), misc, MCORR)
    drive, head = leaf[0], leaf[1]

    e, h = drive, head
    spot = [0]
    for k in range(levels):
        m = steps >> (k + 1)
        (el, er), (hl, hr) = halves(e, m), halves(h, m)
        el2, hr2 = split(el), split(hr)
        e = er + step(el2, k, KP)
        h = hl + step(beside(el2, hr2), k, KU)
        here = pl.ds(spot[-1], el.shape[0])
        kept[0, here, :] = el
        kept[1, here, :] = hr + step(el2, k, KW)
        spot.append(spot[-1] + el.shape[0])

    half = ns // 2
    for ref in (mine, ends.at[place]):
        ref[0:1, :] = e[0:1, :half]
        ref[1:2, :] = e[0:1, half:]
        ref[2:3, :] = h[0:1, :half]
        ref[3:4, :] = h[0:1, half:]

    def end_copy(k):
        return pltpu.make_async_remote_copy(
            src_ref=mine,
            dst_ref=ends.at[place],
            send_sem=esend_sem.at[k],
            recv_sem=erecv_sem.at[k],
            device_id=target(k),
            device_id_type=MESH,
        )

    def end_arrival(k):
        q = lax.rem(place - k + n, n)
        return pltpu.make_async_remote_copy(
            src_ref=mine,
            dst_ref=ends.at[q],
            send_sem=esend_sem.at[k],
            recv_sem=erecv_sem.at[k],
            device_id=target(k),
            device_id_type=MESH,
        )

    def send_end(k, c):
        end_copy(k).start()
        return c

    lax.fori_loop(1, n, send_end, 0)

    def take_end(k, c):
        end_arrival(k).wait_recv()
        return c

    lax.fori_loop(1, n, take_end, 0)

    x = jnp.concatenate([ends[:, 0, :], ends[:, 1, :]], axis=1)
    s = jnp.concatenate([ends[:, 2, :], ends[:, 3, :]], axis=1)
    for k in range(dev_levels):
        x = x + shift_down(mul(split(x), dev, k, 0), 1 << k)
    x2 = split(x)
    last = lax.broadcasted_iota(jnp.int32, (n, 1), 0) == n - 1
    s = s + shift_down(mul(x2, misc, MWIN), 1) + jnp.where(last, mul(x2, misc, MEXIT), 0.0)
    for k in range(dev_levels):
        s = s + shift_up(mul(split(s), dev, k, 1), 1 << k)
    pick[0] = shift_down(x, 1)
    pick[1] = jnp.where(last, mul(x2, misc, MMODEL), shift_up(s, 1))
    x = first_rows(jnp.broadcast_to(pick[0, pl.ds(place, 1), :], (16, ns)), 1)
    s = first_rows(jnp.broadcast_to(pick[1, pl.ds(place, 1), :], (16, ns)), 1)

    for k in range(levels - 1, -1, -1):
        m = steps >> (k + 1)
        here = pl.ds(spot[k], spot[k + 1] - spot[k])
        el, g = kept[0, here, :], kept[1, here, :]
        x2, s2 = split(x), split(s)
        xr = el + step(x2, k, KP)
        sl = g + step(beside(s2, x2), k, KQ)
        x = stack(x, xr, m)
        s = stack(sl, s, m)
    x2 = split(x)
    f_rows = leaf[0] + step(x2, 0, KP)
    s_rows = leaf[1] + (step(x2, 0, KW) + step(split(s), 0, KQ))
    for t in range(steps):
        r = bit_reversed(t, levels)
        filtered[t : t + 1, :] = f_rows[r : r + 1, :]
        smoothed[t : t + 1, :] = s_rows[r : r + 1, :]

    def drain(k, c):
        rs_copy(k).wait_send()
        return c

    lax.fori_loop(0, n_in - 1, drain, 0)

    def drain_end(k, c):
        end_copy(k).wait_send()
        return c

    lax.fori_loop(1, n, drain_end, 0)


def on_device(
    readings, obs_rows, obs_block, sensor_prec, prior_mean, filt_trans, model_trans, info_gain, smooth_gain
):
    n_out, n_in = lax.axis_size("outer"), lax.axis_size("inner")
    n = n_out * n_in
    rows, sensors = readings.shape
    steps = rows // n_in
    ns = filt_trans.shape[0]
    blk = obs_rows.shape[1]
    total = obs_rows.shape[0]
    levels = steps.bit_length() - 1
    dev_levels = n.bit_length() - 1
    vmem = pl.BlockSpec(memory_space=pltpu.VMEM)
    hbm = pl.BlockSpec(memory_space=pl.ANY)
    dma = pltpu.SemaphoreType.DMA
    return pl.pallas_call(
        functools.partial(kernel, n_out, n_in),
        out_shape=[jax.ShapeDtypeStruct((steps, ns), F32)] * 2,
        in_specs=[hbm, hbm] + [vmem] * 7,
        out_specs=[vmem, vmem],
        scratch_shapes=[
            pltpu.VMEM((n_in, steps, sensors), F32),
            pltpu.VMEM((blk, sensors), F32),
            pltpu.VMEM((2, sensors, ns), BF16),
            pltpu.VMEM((n_in, steps, ns), F32),
            pltpu.VMEM((n_in - 1, steps, ns), F32),
            pltpu.VMEM((steps, ns), F32),
            pltpu.VMEM((levels, 2, 5 * ns, ns), BF16),
            pltpu.VMEM((dev_levels, 2, 2, ns, ns), BF16),
            pltpu.VMEM((5, 2, ns, ns), BF16),
            pltpu.VMEM((ns, ns), F32),
            pltpu.VMEM((ns, ns), F32),
            pltpu.VMEM((ns, ns), F32),
            pltpu.VMEM((8, ns // 2), F32),
            pltpu.VMEM((n, 8, ns // 2), F32),
            pltpu.VMEM((2, n, ns), F32),
            pltpu.VMEM((2, steps + 16 * levels, ns), F32),
            pltpu.VMEM((2, steps, ns), F32),
            dma((n_in,)),
            dma(()),
            dma((n_in - 1,)),
            dma((n_in - 1,)),
            dma((n,)),
            dma((n,)),
        ],
        compiler_params=pltpu.CompilerParams(
            collective_id=0, has_side_effects=True, vmem_limit_bytes=56 * 1024 * 1024
        ),
        name="smoother",
    )(
        readings,
        obs_rows.T,
        obs_block.reshape(total // 128, 128),
        sensor_prec.reshape(total // 128, 128),
        prior_mean.reshape(1, ns),
        filt_trans,
        model_trans,
        info_gain,
        smooth_gain,
    )


def solution(mesh):
    placed = (P(("groups", "outer"), "inner"), P(), P(), P(), P("groups"), P(), P(), P(), P())
    return jax.shard_map(
        on_device,
        mesh=mesh,
        in_specs=placed,
        out_specs=(P(("groups", "outer", "inner"), None), P(("groups", "outer", "inner"), None)),
        check_vma=False,
    )
```
